512 devices in a mesh: row: 16 (over x_lo, y), col: 32 (over x_hi, z, core).
Axes of the slice: x: 4 (x_hi: 2, x_lo: 2; x = x_hi * 2 + x_lo), y: 8, z: 8, core: 2. Of those that a mesh axis runs over, the one named last changes fastest.
Arguments:
- sensitivity: bfloat16 [24576, 16384], P('row', 'col'), may hold values from -1.5 to 1.5
- stencil_weights: float32 [4], replicated, may hold values from 0.1 to 0.6
- cell_offsets: int32 [3], replicated, may hold values from 1 to 64, as said below
- step_start: int32 [1], replicated, may hold values from 0 to 1023
Outputs:
- gram_columns: bfloat16 [32, 24576, 768], P('col', 'row')
The draws below stay inside these ranges and needn't reach their ends.
Inputs may be any that keep to these rules, and one draw needn't show every extreme that they name: `cell_offsets`: every offset lies between 1 and 64, and one of them equals 64.
All inputs are finite; a program needn't handle non-finite values.
Results may differ from the reference program's by a relative error of at most 0.0049.
Values may be sent and summed in bfloat16 or wider, within the bound.
No kernel may reach another device: no remote copies, remote signals or barrier semaphores. Data moves between devices by JAX's collectives and lax.ppermute only.
A program may use at most 64 MiB of HBM per device.

```python
import jax
import jax.numpy as jnp
from jax import lax

DROWS_DEV = 48
CELLS_DEV = 512
HALO = 64
NOFF = 3
STEPS = 2
BLOCK_ROWS = 1536
NDATA = 24576
NCELL = 16384
N_ROW = 16
N_COL = 32


def draw_cell_offsets(key, part):
    values = jax.random.randint(jax.random.fold_in(key, 11), (NOFF,), 1, HALO + 1)
    place = jax.random.randint(jax.random.fold_in(key, 12), (), 0, NOFF)
    marked = jnp.arange(NOFF) == place
    return jnp.where(marked, HALO, values).astype(jnp.int32)


def steps_of(key, dims, split, low, top_value):
    gain, own = 1.0, jax.random.fold_in(key, 6)
    for dim, blocks in split:
        draws = jnp.exp(jax.random.uniform(jax.random.fold_in(own, dim), (blocks,), jnp.float32, low / len(split), top_value / len(split)))
        gain = gain * jnp.repeat(draws, dims[dim] // blocks).reshape([-1 if axis == dim else 1 for axis in range(len(dims))])
    return gain


def gaussian(rng, extent, deviation, limit, pieces=(), kind=jnp.bfloat16):
    gain = steps_of(rng, extent, pieces, -0.22, 0.18) if pieces else 1.0
    entries = jax.random.normal(rng, extent, jnp.float32) * deviation * gain
    return jnp.minimum(jnp.maximum(entries, -limit), limit).astype(kind)


def setup_inputs(seed: int = 0) -> dict:
    keys = jax.random.split(jax.random.key(seed), 5)
    sensitivity = gaussian(keys[0], (NDATA, NCELL), 0.25, 1.5, ((0, 16), (1, 32)))
    stencil_weights = jnp.clip(jax.random.uniform(keys[1], (NOFF + 1,), jnp.float32, 0.1, 0.6), 0.1, 0.6)
    cell_offsets = draw_cell_offsets(jax.random.fold_in(keys[4], 71), 0)
    step_start = jax.random.randint(keys[3], (1,), 0, 1024).astype(jnp.int32)
    return dict(sensitivity=sensitivity, stencil_weights=stencil_weights, cell_offsets=cell_offsets, step_start=step_start)


def smooth_block(window, cell_offsets, stencil_weights, width):
    widened = window.astype(jnp.float32)
    center = lax.slice_in_dim(widened, HALO, HALO + width, axis=1)
    total = stencil_weights[0] * center
    for term in range(NOFF):
        forward = lax.dynamic_slice_in_dim(widened, HALO + cell_offsets[term], width, 1)
        backward = lax.dynamic_slice_in_dim(widened, HALO - cell_offsets[term], width, 1)
        total = total + stencil_weights[term + 1] * (forward + backward)
    return total.astype(jnp.bfloat16)


def reference(sensitivity, stencil_weights, cell_offsets, step_start):
    padded = jnp.pad(sensitivity, ((0, 0), (HALO, HALO)))

    def one_block(block_index):
        rows = lax.dynamic_slice_in_dim(padded, block_index * BLOCK_ROWS, BLOCK_ROWS, 0)
        total = jnp.zeros((BLOCK_ROWS, NDATA), jnp.float32)
        for step in range(STEPS):
            owner = ((STEPS * block_index + step_start[0] + step) % N_COL).astype(jnp.int32)
            window = lax.dynamic_slice_in_dim(rows, owner * CELLS_DEV, CELLS_DEV + 2 * HALO, 1)
            smoothed = smooth_block(window, cell_offsets, stencil_weights, CELLS_DEV)
            columns = lax.dynamic_slice_in_dim(sensitivity, owner * CELLS_DEV, CELLS_DEV, 1)
            total = total + lax.dot_general(smoothed, columns, (((1,), (1,)), ((), ())),
                                            preferred_element_type=jnp.float32)
        grouped = total.astype(jnp.bfloat16).reshape(BLOCK_ROWS, N_ROW, N_COL, DROWS_DEV)
        return grouped.transpose(2, 0, 1, 3).reshape(N_COL, BLOCK_ROWS, N_ROW * DROWS_DEV)

    stacked = lax.map(one_block, jnp.arange(N_ROW, dtype=jnp.int32))
    return stacked.transpose(1, 0, 2, 3).reshape(N_COL, NDATA, N_ROW * DROWS_DEV)
```

```python
import jax
import jax.numpy as jnp
from jax import lax
from jax.experimental import pallas as pl
from jax.experimental.pallas import tpu as pltpu
from jax.sharding import PartitionSpec as P

HALO = 64
NOFF = 3
STEPS = 2
N_XH = 2
N_Z = 8
N_C = 2
LANE = 128
VMEM_LIMIT = 20 * 1024 * 1024


def select_kernel(start_ref, offsets_ref, weights_ref, own_ref, chosen_ref, piece_ref, window, sem, wsem):
    count, rows, cells = own_ref.shape
    start = lax.rem(start_ref[0], count)
    copies = []
    first = lax.rem(STEPS * lax.axis_index("row") + start, count)
    for j in range(4):
        block = lax.rem(first + (j - 1 + count), count)
        copy = pltpu.make_async_copy(own_ref.at[block], window.at[j], wsem.at[j])
        copy.start()
        copies.append(copy)
    moves = []
    for t in range(count):
        block = lax.rem(t + start, count)
        move = pltpu.make_async_copy(own_ref.at[block], chosen_ref.at[t // STEPS, t % STEPS], sem.at[t])
        move.start()
        moves.append(move)
    for copy in copies:
        copy.wait()
    for s in range(STEPS):
        here = lax.rem(first + s, count)
        before = jnp.where(here > 0, window[s][:, cells - LANE:].astype(jnp.float32), 0.0)
        after = jnp.where(here < count - 1, window[s + 2][:, :LANE].astype(jnp.float32), 0.0)
        center = window[s + 1].astype(jnp.float32)
        wide = jnp.concatenate([before, center, after], axis=1)
        width = cells + 2 * LANE
        total = weights_ref[0] * center
        for m in range(NOFF):
            offset = offsets_ref[m]
            forward = pltpu.roll(wide, width - offset, 1)[:, LANE:LANE + cells]
            backward = pltpu.roll(wide, offset, 1)[:, LANE:LANE + cells]
            total = total + weights_ref[m + 1] * (forward + backward)
        piece_ref[:, s * cells:(s + 1) * cells] = total.astype(jnp.bfloat16)
    for move in moves:
        move.wait()


def select(own, stencil_weights, cell_offsets, step_start):
    count, rows, cells = own.shape
    smem = pl.BlockSpec(memory_space=pltpu.SMEM)
    return pl.pallas_call(
        select_kernel,
        out_shape=(
            jax.ShapeDtypeStruct((count // STEPS, STEPS, rows, cells), own.dtype),
            jax.ShapeDtypeStruct((rows, STEPS * cells), own.dtype),
        ),
        in_specs=[smem, smem, smem, pl.BlockSpec(memory_space=pl.ANY)],
        out_specs=(pl.BlockSpec(memory_space=pl.ANY), pl.BlockSpec(memory_space=pltpu.VMEM)),
        scratch_shapes=[
            pltpu.VMEM((4, rows, cells), own.dtype),
            pltpu.SemaphoreType.DMA((count,)),
            pltpu.SemaphoreType.DMA((4,)),
        ],
    )(step_start, cell_offsets, stencil_weights, own)


def gram_kernel(*refs):
    pieces, right_ref, out_ref, left, right, sem, rsem = refs[:9], refs[9], refs[10], *refs[11:]
    tile = pl.program_id(0)
    tile_rows = out_ref.shape[0]
    cells = right.shape[3]
    piece = pieces[0].shape[-2]

    def copies():
        column = lax.axis_index("col")
        xh = column // (N_Z * N_C)
        z = lax.rem(column // N_C, N_Z)
        core = lax.rem(column, N_C)
        up = 1 - 2 * core
        made = []
        n = 0
        for index, ref in enumerate(pieces):
            hop = index if index < 5 else index - 4
            side = 0 if index < 5 else 1
            toward = up if side == 0 else -up
            source_z = lax.rem(z - hop * toward + N_Z, N_Z)
            source_core = core if side == 0 else 1 - core
            for rc in range(N_C if hop < 4 else 1):
                for rx in range(N_XH):
                    from_core = source_core if rc == 0 else 1 - source_core
                    from_xh = xh if rx == 0 else 1 - xh
                    place = (from_xh * N_Z + source_z) * N_C + from_core
                    source = ref.at[rc, rx] if hop < 4 else ref.at[rx]
                    target = left.at[pl.ds(pl.multiple_of(place * piece, piece), piece)]
                    made.append(pltpu.make_async_copy(source, target, sem.at[n]))
                    n += 1
        for s in range(STEPS):
            made.append(pltpu.make_async_copy(right_ref.at[:, s], right.at[s], rsem.at[s]))
        return made

    @pl.when(tile == 0)
    def _():
        made = copies()
        for copy in made:
            copy.start()
        for copy in made:
            copy.wait()

    rows = left[pl.ds(pl.multiple_of(tile * tile_rows, tile_rows), tile_rows), :]
    total = None
    for s in range(STEPS):
        columns = right[s].reshape(-1, cells)
        part = lax.dot_general(
            rows[:, s * cells:(s + 1) * cells], columns,
            (((1,), (1,)), ((), ())), preferred_element_type=jnp.float32,
        )
        total = part if total is None else total + part
    out_ref[...] = total.astype(out_ref.dtype)


def gram(pieces, right, rows_dev):
    row_count, steps, piece, cells = right.shape
    width = row_count * piece
    tiles = 4
    return pl.pallas_call(
        gram_kernel,
        out_shape=jax.ShapeDtypeStruct((rows_dev, width), jnp.bfloat16),
        grid=(tiles,),
        in_specs=[pl.BlockSpec(memory_space=pl.ANY)] * 10,
        out_specs=pl.BlockSpec((rows_dev // tiles, width), lambda t: (t, 0)),
        scratch_shapes=[
            pltpu.VMEM((rows_dev, steps * cells), jnp.bfloat16),
            pltpu.VMEM((steps, row_count, piece, cells), jnp.bfloat16),
            pltpu.SemaphoreType.DMA((32,)),
            pltpu.SemaphoreType.DMA((steps,)),
        ],
        compiler_params=pltpu.CompilerParams(vmem_limit_bytes=VMEM_LIMIT),
    )(*pieces, right)


def place(xh, z, core):
    return ((xh % N_XH) * N_Z + z % N_Z) * N_C + core % N_C


PLACES = [(xh, z, core) for xh in range(N_XH) for z in range(N_Z) for core in range(N_C)]
SWAP_X = [(place(x, z, c), place(x + 1, z, c)) for x, z, c in PLACES]
SWAP_CORE = [(place(x, z, c), place(x, z, c + 1)) for x, z, c in PLACES]
RING = [(place(x, z, c), place(x, z + 1 - 2 * c, c)) for x, z, c in PLACES]


def gather_left(piece):
    both_x = jnp.stack([piece, lax.ppermute(piece, "col", SWAP_X)])
    base = jnp.stack([both_x, lax.ppermute(both_x, "col", SWAP_CORE)])
    held, other = [], []
    block = base
    for hop in range(1, 5):
        block = lax.ppermute(block if hop < 4 else block[0], "col", RING)
        held.append(block)
        other.append(lax.ppermute(block, "col", SWAP_CORE))
    return [base] + held + other


def local(sensitivity, stencil_weights, cell_offsets, step_start):
    rows_dev, cells_dev = sensitivity.shape
    col_count = lax.axis_size("col")
    piece_rows = rows_dev // col_count
    blocks = sensitivity.reshape(col_count, piece_rows, cells_dev)
    own = lax.all_to_all(blocks, "col", split_axis=0, concat_axis=0, tiled=True)
    chosen, piece = select(own, stencil_weights, cell_offsets, step_start)
    right = lax.all_to_all(chosen, "row", split_axis=0, concat_axis=0, tiled=True)
    pieces = gather_left(piece)
    return gram(pieces, right, rows_dev)[None]


def solution(mesh):
    in_specs = (P("row", "col"), P(), P(), P())
    out_specs = P("col", "row", None)
    return jax.shard_map(local, mesh=mesh, in_specs=in_specs, out_specs=out_specs, check_vma=False)
```

```python
import jax
import jax.numpy as jnp
from jax import lax
from jax.experimental import pallas as pl
from jax.experimental.pallas import tpu as pltpu
from jax.sharding import PartitionSpec as P

HALO = 64
NOFF = 3
STEPS = 2
N_XH = 2
N_Z = 8
N_C = 2
LANE = 128
VMEM_LIMIT = 16 * 1024 * 1024
SELECT_LIMIT = 10 * 1024 * 1024


def select_kernel(start_ref, offsets_ref, weights_ref, own_ref, chosen_ref, piece_ref):
    count, rows, cells = own_ref.shape
    start = lax.rem(start_ref[0], count)
    first = lax.rem(STEPS * lax.axis_index("row") + start, count)
    for s in range(STEPS):
        here = lax.rem(first + s, count)
        left = own_ref[lax.rem(here + count - 1, count)][:, cells - LANE:].astype(jnp.float32)
        right = own_ref[lax.rem(here + 1, count)][:, :LANE].astype(jnp.float32)
        before = jnp.where(here > 0, left, 0.0)
        after = jnp.where(here < count - 1, right, 0.0)
        center = own_ref[here].astype(jnp.float32)
        wide = jnp.concatenate([before, center, after], axis=1)
        width = cells + 2 * LANE
        total = weights_ref[0] * center
        for m in range(NOFF):
            offset = offsets_ref[m]
            forward = pltpu.roll(wide, width - offset, 1)[:, LANE:LANE + cells]
            backward = pltpu.roll(wide, offset, 1)[:, LANE:LANE + cells]
            total = total + weights_ref[m + 1] * (forward + backward)
        piece_ref[:, s * cells:(s + 1) * cells] = total.astype(jnp.bfloat16)

    @pl.loop(0, count)
    def _(t):
        chosen_ref[t // STEPS, lax.rem(t, STEPS)] = own_ref[lax.rem(t + start, count)]


def select(own, stencil_weights, cell_offsets, step_start):
    count, rows, cells = own.shape
    smem = pl.BlockSpec(memory_space=pltpu.SMEM)
    vmem = pl.BlockSpec(memory_space=pltpu.VMEM)
    return pl.pallas_call(
        select_kernel,
        out_shape=(
            jax.ShapeDtypeStruct((count // STEPS, STEPS, rows, cells), own.dtype),
            jax.ShapeDtypeStruct((rows, STEPS * cells), own.dtype),
        ),
        in_specs=[smem, smem, smem, vmem],
        out_specs=(vmem, vmem),
        compiler_params=pltpu.CompilerParams(vmem_limit_bytes=SELECT_LIMIT),
    )(step_start, cell_offsets, stencil_weights, own)


PAIR = [[(hop, 0, 0), (hop, 0, 1)] for hop in range(4)]
PAIR_X = [[(hop, 1, 0), (hop, 1, 1)] for hop in range(4)]
LAST = [(4, 0, 0), (4, 1, 0), (0, 1, 0)]


def gram_kernel(*refs):
    count = len(LAYOUT)
    pieces, right_ref, out_ref, left, right, sem, rsem = refs[:count], refs[count], refs[count + 1], *refs[count + 2:]
    tile = pl.program_id(0)
    tile_rows = out_ref.shape[0]
    cells = right.shape[3]
    piece = right.shape[2]

    def copies():
        column = lax.axis_index("col")
        xh = column // (N_Z * N_C)
        z = lax.rem(column // N_C, N_Z)
        core = lax.rem(column, N_C)
        made = []
        n = 0
        for ref, (side, holds) in zip(pieces, LAYOUT):
            side_core = core if side == 0 else 1 - core
            up = 1 - 2 * side_core
            for index, (hop, other_x, other_core) in enumerate(holds):
                from_z = lax.rem(z - hop * up + N_Z, N_Z)
                from_core = 1 - side_core if other_core else side_core
                from_xh = 1 - xh if other_x else xh
                at = ((from_xh * N_Z + from_z) * N_C + from_core) * piece
                target = left.at[pl.ds(pl.multiple_of(at, piece), piece)]
                made.append(pltpu.make_async_copy(ref.at[index], target, sem.at[n]))
                n += 1
        for s in range(STEPS):
            made.append(pltpu.make_async_copy(right_ref.at[:, s], right.at[s], rsem.at[s]))
        return made

    @pl.when(tile == 0)
    def _():
        made = copies()
        for copy in made:
            copy.start()
        for copy in made:
            copy.wait()

    rows = left[pl.ds(pl.multiple_of(tile * tile_rows, tile_rows), tile_rows), :]
    total = None
    for s in range(STEPS):
        columns = right[s].reshape(-1, cells)
        part = lax.dot_general(
            rows[:, s * cells:(s + 1) * cells], columns,
            (((1,), (1,)), ((), ())), preferred_element_type=jnp.float32,
        )
        total = part if total is None else total + part
    out_ref[...] = total.astype(out_ref.dtype)


def gram(pieces, right, rows_dev):
    row_count, steps, piece, cells = right.shape
    width = row_count * piece
    tiles = 4
    return pl.pallas_call(
        gram_kernel,
        out_shape=jax.ShapeDtypeStruct((rows_dev, width), jnp.bfloat16),
        grid=(tiles,),
        in_specs=[pl.BlockSpec(memory_space=pl.ANY)] * (len(LAYOUT) + 1),
        out_specs=pl.BlockSpec((rows_dev // tiles, width), lambda t: (t, 0)),
        scratch_shapes=[
            pltpu.VMEM((rows_dev, steps * cells), jnp.bfloat16),
            pltpu.VMEM((steps, row_count, piece, cells), jnp.bfloat16),
            pltpu.SemaphoreType.DMA((32,)),
            pltpu.SemaphoreType.DMA((steps,)),
        ],
        compiler_params=pltpu.CompilerParams(vmem_limit_bytes=VMEM_LIMIT),
    )(*pieces, right)


def place(xh, z, core):
    return ((xh % N_XH) * N_Z + z % N_Z) * N_C + core % N_C


PLACES = [(xh, z, core) for xh in range(N_XH) for z in range(N_Z) for core in range(N_C)]
SWAP_X = [(place(x, z, c), place(x + 1, z, c)) for x, z, c in PLACES]
SWAP_CORE = [(place(x, z, c), place(x, z, c + 1)) for x, z, c in PLACES]
RING = [[(place(x, z, c), place(x, z + hop * (1 - 2 * c), c)) for x, z, c in PLACES] for hop in range(5)]
LAYOUT = (
    [(0, PAIR[0])]
    + [(0, PAIR[hop]) for hop in (1, 2, 3)]
    + [(0, PAIR_X[hop]) for hop in (1, 2, 3)]
    + [(0, LAST)]
    + [(1, PAIR[hop] + PAIR_X[hop]) for hop in (1, 2, 3)]
    + [(1, LAST)]
)


def gather_left(piece):
    def swap_x(block):
        return lax.ppermute(block, "col", SWAP_X)

    def swap_core(block):
        return lax.ppermute(block, "col", SWAP_CORE)

    pair = jnp.stack([piece, swap_core(piece)])
    far = lax.ppermute(piece, "col", RING[4])
    near = [lax.ppermute(pair, "col", RING[hop]) for hop in (3, 2, 1)][::-1]
    across = [swap_x(block) for block in near]
    last = jnp.stack([far, swap_x(far), swap_x(piece)])
    other = [swap_core(jnp.concatenate([here, there])) for here, there in zip(near, across)]
    return [pair] + near + across + [last] + other + [swap_core(last)]


def local(sensitivity, stencil_weights, cell_offsets, step_start):
    rows_dev, cells_dev = sensitivity.shape
    col_count = lax.axis_size("col")
    piece_rows = rows_dev // col_count
    blocks = sensitivity.reshape(col_count, piece_rows, cells_dev)
    own = lax.all_to_all(blocks, "col", split_axis=0, concat_axis=0, tiled=True)
    chosen, piece = select(own, stencil_weights, cell_offsets, step_start)
    right = lax.all_to_all(chosen, "row", split_axis=0, concat_axis=0, tiled=True)
    pieces = gather_left(piece)
    return gram(pieces, right, rows_dev)[None]


def solution(mesh):
    in_specs = (P("row", "col"), P(), P(), P())
    out_specs = P("col", "row", None)
    return jax.shard_map(local, mesh=mesh, in_specs=in_specs, out_specs=out_specs, check_vma=False)
```

```python
import jax
import jax.numpy as jnp
from jax import lax
from jax.experimental import pallas as pl
from jax.experimental.pallas import tpu as pltpu
from jax.sharding import PartitionSpec as P

HALO = 64
NOFF = 3
STEPS = 2
N_XH = 2
N_Z = 8
N_C = 2
LANE = 128
VMEM_LIMIT = 16 * 1024 * 1024
SELECT_LIMIT = 10 * 1024 * 1024


def select_kernel(start_ref, offsets_ref, weights_ref, own_ref, chosen_ref, piece_ref):
    count, rows, cells = own_ref.shape
    start = lax.rem(start_ref[0], count)
    first = lax.rem(STEPS * lax.axis_index("row") + start, count)
    for s in range(STEPS):
        here = lax.rem(first + s, count)
        left = own_ref[lax.rem(here + count - 1, count)][:, cells - LANE:].astype(jnp.float32)
        right = own_ref[lax.rem(here + 1, count)][:, :LANE].astype(jnp.float32)
        before = jnp.where(here > 0, left, 0.0)
        after = jnp.where(here < count - 1, right, 0.0)
        center = own_ref[here].astype(jnp.float32)
        wide = jnp.concatenate([before, center, after], axis=1)
        width = cells + 2 * LANE
        total = weights_ref[0] * center
        for m in range(NOFF):
            offset = offsets_ref[m]
            forward = pltpu.roll(wide, width - offset, 1)[:, LANE:LANE + cells]
            backward = pltpu.roll(wide, offset, 1)[:, LANE:LANE + cells]
            total = total + weights_ref[m + 1] * (forward + backward)
        piece_ref[:, s * cells:(s + 1) * cells] = total.astype(jnp.bfloat16)

    @pl.loop(0, count)
    def _(t):
        chosen_ref[t // STEPS, lax.rem(t, STEPS)] = own_ref[lax.rem(t + start, count)]


def select(own, stencil_weights, cell_offsets, step_start):
    count, rows, cells = own.shape
    smem = pl.BlockSpec(memory_space=pltpu.SMEM)
    vmem = pl.BlockSpec(memory_space=pltpu.VMEM)
    return pl.pallas_call(
        select_kernel,
        out_shape=(
            jax.ShapeDtypeStruct((count // STEPS, STEPS, rows, cells), own.dtype),
            jax.ShapeDtypeStruct((rows, STEPS * cells), own.dtype),
        ),
        in_specs=[smem, smem, smem, vmem],
        out_specs=(vmem, vmem),
        compiler_params=pltpu.CompilerParams(vmem_limit_bytes=SELECT_LIMIT),
    )(step_start, cell_offsets, stencil_weights, own)


def gram_kernel(*refs):
    count = len(LAYOUT)
    pieces, right_ref, out_ref, left = refs[:count], refs[count], refs[count + 1], refs[count + 2]
    tile = pl.program_id(0)
    tile_rows = out_ref.shape[0]
    row_count, steps, piece, cells = right_ref.shape

    @pl.when(tile == 0)
    def _():
        column = lax.axis_index("col")
        xh = column // (N_Z * N_C)
        z = lax.rem(column // N_C, N_Z)
        core = lax.rem(column, N_C)
        for ref, (side, holds) in zip(pieces, LAYOUT):
            side_core = core if side == 0 else 1 - core
            up = 1 - 2 * side_core
            for index, (hop, other_x, other_core) in enumerate(holds):
                from_z = lax.rem(z - hop * up + N_Z, N_Z)
                from_core = 1 - side_core if other_core else side_core
                from_xh = 1 - xh if other_x else xh
                at = ((from_xh * N_Z + from_z) * N_C + from_core) * piece
                left[pl.ds(pl.multiple_of(at, piece), piece), :] = ref[index]

    rows = left[pl.ds(pl.multiple_of(tile * tile_rows, tile_rows), tile_rows), :]
    total = None
    for s in range(steps):
        columns = right_ref[:, s].reshape(row_count * piece, cells)
        part = lax.dot_general(
            rows[:, s * cells:(s + 1) * cells], columns,
            (((1,), (1,)), ((), ())), preferred_element_type=jnp.float32,
        )
        total = part if total is None else total + part
    out_ref[...] = total.astype(out_ref.dtype)


def gram(pieces, right, rows_dev):
    row_count, steps, piece, cells = right.shape
    width = row_count * piece
    tiles = 4
    return pl.pallas_call(
        gram_kernel,
        out_shape=jax.ShapeDtypeStruct((rows_dev, width), jnp.bfloat16),
        grid=(tiles,),
        in_specs=[pl.BlockSpec(memory_space=pltpu.VMEM)] * (len(LAYOUT) + 1),
        out_specs=pl.BlockSpec((rows_dev // tiles, width), lambda t: (t, 0)),
        scratch_shapes=[pltpu.VMEM((rows_dev, steps * cells), jnp.bfloat16)],
        compiler_params=pltpu.CompilerParams(vmem_limit_bytes=VMEM_LIMIT),
    )(*pieces, right)


def place(xh, z, core):
    return ((xh % N_XH) * N_Z + z % N_Z) * N_C + core % N_C


PLACES = [(xh, z, core) for xh in range(N_XH) for z in range(N_Z) for core in range(N_C)]
SWAP_X = [(place(x, z, c), place(x + 1, z, c)) for x, z, c in PLACES]
SWAP_CORE = [(place(x, z, c), place(x, z, c + 1)) for x, z, c in PLACES]
RING = [[(place(x, z, c), place(x, z + hop * (1 - 2 * c), c)) for x, z, c in PLACES] for hop in range(5)]
OWN, FIRST, FAR = [(0, 0, 0)], [(1, 0, 0), (1, 0, 1)], [(4, 0, 0)]
SECOND = [(2, 0, 0), (2, 0, 1), (3, 0, 0), (3, 0, 1)]


def across(holds):
    return [(hop, 1, core) for hop, _, core in holds]


LAYOUT = [
    (0, [(0, 0, 0), (0, 0, 1)]),
    (0, FIRST),
    (0, FAR),
    (0, SECOND),
    (0, across(OWN + FIRST + FAR)),
    (0, across(SECOND)),
    (1, FIRST + FAR + across(OWN + FIRST + FAR)),
    (1, SECOND),
    (1, across(SECOND)),
]


def gather_left(piece):
    def swap_x(block):
        return lax.ppermute(block, "col", SWAP_X)

    def swap_core(block):
        return lax.ppermute(block, "col", SWAP_CORE)

    own = piece[None]
    pair = jnp.concatenate([own, swap_core(own)])
    far = lax.ppermute(own, "col", RING[4])
    first = lax.ppermute(pair, "col", RING[1])
    second = lax.ppermute(jnp.concatenate([pair, first]), "col", RING[2])
    near = jnp.concatenate([first, far])
    near_x = swap_x(jnp.concatenate([own, near]))
    second_x = swap_x(second)
    return [
        pair, first, far, second, near_x, second_x,
        swap_core(jnp.concatenate([near, near_x])), swap_core(second), swap_core(second_x),
    ]


def local(sensitivity, stencil_weights, cell_offsets, step_start):
    rows_dev, cells_dev = sensitivity.shape
    col_count = lax.axis_size("col")
    piece_rows = rows_dev // col_count
    blocks = sensitivity.reshape(col_count, piece_rows, cells_dev)
    own = lax.all_to_all(blocks, "col", split_axis=0, concat_axis=0, tiled=True)
    chosen, piece = select(own, stencil_weights, cell_offsets, step_start)
    right = lax.all_to_all(chosen, "row", split_axis=0, concat_axis=0, tiled=True)
    pieces = gather_left(piece)
    return gram(pieces, right, rows_dev)[None]


def solution(mesh):
    in_specs = (P("row", "col"), P(), P(), P())
    out_specs = P("col", "row", None)
    return jax.shard_map(local, mesh=mesh, in_specs=in_specs, out_specs=out_specs, check_vma=False)
```

```python
import jax
import jax.numpy as jnp
from jax import lax
from jax.experimental import pallas as pl
from jax.experimental.pallas import tpu as pltpu
from jax.sharding import PartitionSpec as P

HALO = 64
NOFF = 3
STEPS = 2
N_XH = 2
N_Z = 8
N_C = 2
LANE = 128
VMEM_LIMIT = 16 * 1024 * 1024
SELECT_LIMIT = 10 * 1024 * 1024
ASSEMBLE_LIMIT = 12 * 1024 * 1024


def select_kernel(start_ref, offsets_ref, weights_ref, own_ref, chosen_ref, piece_ref):
    count, rows, cells = own_ref.shape
    start = lax.rem(start_ref[0], count)
    first = lax.rem(STEPS * lax.axis_index("row") + start, count)
    for s in range(STEPS):
        here = lax.rem(first + s, count)
        left = own_ref[lax.rem(here + count - 1, count)][:, cells - LANE:].astype(jnp.float32)
        right = own_ref[lax.rem(here + 1, count)][:, :LANE].astype(jnp.float32)
        before = jnp.where(here > 0, left, 0.0)
        after = jnp.where(here < count - 1, right, 0.0)
        center = own_ref[here].astype(jnp.float32)
        wide = jnp.concatenate([before, center, after], axis=1)
        width = cells + 2 * LANE
        total = weights_ref[0] * center
        for m in range(NOFF):
            offset = offsets_ref[m]
            forward = pltpu.roll(wide, width - offset, 1)[:, LANE:LANE + cells]
            backward = pltpu.roll(wide, offset, 1)[:, LANE:LANE + cells]
            total = total + weights_ref[m + 1] * (forward + backward)
        piece_ref[:, s * cells:(s + 1) * cells] = total.astype(jnp.bfloat16)

    @pl.loop(0, count)
    def _(t):
        chosen_ref[t // STEPS, lax.rem(t, STEPS)] = own_ref[lax.rem(t + start, count)]


def select(own, stencil_weights, cell_offsets, step_start):
    count, rows, cells = own.shape
    smem = pl.BlockSpec(memory_space=pltpu.SMEM)
    vmem = pl.BlockSpec(memory_space=pltpu.VMEM)
    return pl.pallas_call(
        select_kernel,
        out_shape=(
            jax.ShapeDtypeStruct((count // STEPS, STEPS, rows, cells), own.dtype),
            jax.ShapeDtypeStruct((rows, STEPS * cells), own.dtype),
        ),
        in_specs=[smem, smem, smem, vmem],
        out_specs=(vmem, vmem),
        compiler_params=pltpu.CompilerParams(vmem_limit_bytes=SELECT_LIMIT),
    )(step_start, cell_offsets, stencil_weights, own)


def placed(layout):
    column = lax.axis_index("col")
    xh = column // (N_Z * N_C)
    z = lax.rem(column // N_C, N_Z)
    core = lax.rem(column, N_C)
    for array, (side, holds) in enumerate(layout):
        side_core = core if side == 0 else 1 - core
        up = 1 - 2 * side_core
        for index, (hop, other_x, other_core) in enumerate(holds):
            from_z = lax.rem(z - hop * up + N_Z, N_Z)
            from_core = 1 - side_core if other_core else side_core
            from_xh = 1 - xh if other_x else xh
            yield array, index, (from_xh * N_Z + from_z) * N_C + from_core


def assemble_kernel(*refs):
    pieces, left = refs[:-1], refs[-1]
    piece = pieces[0].shape[1]
    for array, index, at in placed(LAYOUT):
        left[pl.ds(pl.multiple_of(at * piece, piece), piece), :] = pieces[array][index]


def assemble(pieces, rows_dev):
    vmem = pl.BlockSpec(memory_space=pltpu.VMEM)
    return pl.pallas_call(
        assemble_kernel,
        out_shape=jax.ShapeDtypeStruct((rows_dev, pieces[0].shape[2]), jnp.bfloat16),
        in_specs=[vmem] * len(pieces),
        out_specs=vmem,
        compiler_params=pltpu.CompilerParams(vmem_limit_bytes=ASSEMBLE_LIMIT),
    )(*pieces)


def gram_kernel(left_ref, right_ref, out_ref):
    tile_rows = out_ref.shape[0]
    row_count, steps, piece, cells = right_ref.shape
    rows = left_ref[pl.ds(pl.multiple_of(pl.program_id(0) * tile_rows, tile_rows), tile_rows), :]
    total = None
    for s in range(steps):
        columns = right_ref[:, s].reshape(row_count * piece, cells)
        part = lax.dot_general(
            rows[:, s * cells:(s + 1) * cells], columns,
            (((1,), (1,)), ((), ())), preferred_element_type=jnp.float32,
        )
        total = part if total is None else total + part
    out_ref[...] = total.astype(out_ref.dtype)


def gram(left, right):
    row_count, steps, piece, cells = right.shape
    rows_dev = left.shape[0]
    width = row_count * piece
    tiles = 4
    vmem = pl.BlockSpec(memory_space=pltpu.VMEM)
    return pl.pallas_call(
        gram_kernel,
        out_shape=jax.ShapeDtypeStruct((rows_dev, width), jnp.bfloat16),
        grid=(tiles,),
        in_specs=[vmem, vmem],
        out_specs=pl.BlockSpec((rows_dev // tiles, width), lambda t: (t, 0)),
        compiler_params=pltpu.CompilerParams(vmem_limit_bytes=VMEM_LIMIT),
    )(left, right)


def place(xh, z, core):
    return ((xh % N_XH) * N_Z + z % N_Z) * N_C + core % N_C


PLACES = [(xh, z, core) for xh in range(N_XH) for z in range(N_Z) for core in range(N_C)]
SWAP_X = [(place(x, z, c), place(x + 1, z, c)) for x, z, c in PLACES]
SWAP_CORE = [(place(x, z, c), place(x, z, c + 1)) for x, z, c in PLACES]
RING = [[(place(x, z, c), place(x, z + hop * (1 - 2 * c), c)) for x, z, c in PLACES] for hop in range(5)]
OWN, FIRST, FAR = [(0, 0, 0)], [(1, 0, 0), (1, 0, 1)], [(4, 0, 0)]
SECOND = [(2, 0, 0), (2, 0, 1), (3, 0, 0), (3, 0, 1)]


def across(holds):
    return [(hop, 1, core) for hop, _, core in holds]


LAYOUT = [
    (0, [(0, 0, 0), (0, 0, 1)]),
    (0, FIRST),
    (0, FAR),
    (0, SECOND),
    (0, across(OWN + FIRST + FAR)),
    (0, across(SECOND)),
    (1, FIRST + FAR + across(OWN + FIRST + FAR)),
    (1, SECOND),
    (1, across(SECOND)),
]


def gather_left(piece):
    def swap_x(block):
        return lax.ppermute(block, "col", SWAP_X)

    def swap_core(block):
        return lax.ppermute(block, "col", SWAP_CORE)

    own = piece[None]
    pair = jnp.concatenate([own, swap_core(own)])
    far = lax.ppermute(own, "col", RING[4])
    first = lax.ppermute(pair, "col", RING[1])
    doubled, first = lax.optimization_barrier((jnp.concatenate([pair, first]), first))
    second = lax.ppermute(doubled, "col", RING[2])
    near = jnp.concatenate([first, far])
    near_x = swap_x(jnp.concatenate([own, near]))
    second_x = swap_x(second)
    return [
        pair, first, far, second, near_x, second_x,
        swap_core(jnp.concatenate([near, near_x])), swap_core(second), swap_core(second_x),
    ]


def local(sensitivity, stencil_weights, cell_offsets, step_start):
    rows_dev, cells_dev = sensitivity.shape
    col_count = lax.axis_size("col")
    piece_rows = rows_dev // col_count
    blocks = sensitivity.reshape(col_count, piece_rows, cells_dev)
    own = lax.all_to_all(blocks, "col", split_axis=0, concat_axis=0, tiled=True)
    chosen, piece = select(own, stencil_weights, cell_offsets, step_start)
    right = lax.all_to_all(chosen, "row", split_axis=0, concat_axis=0, tiled=True)
    pieces = gather_left(piece)
    return gram(assemble(pieces, rows_dev), right)[None]


def solution(mesh):
    in_specs = (P("row", "col"), P(), P(), P())
    out_specs = P("col", "row", None)
    return jax.shard_map(local, mesh=mesh, in_specs=in_specs, out_specs=out_specs, check_vma=False)
```

```python
import jax
import jax.numpy as jnp
from jax import lax
from jax.experimental import pallas as pl
from jax.experimental.pallas import tpu as pltpu
from jax.sharding import PartitionSpec as P

HALO = 64
NOFF = 3
STEPS = 2
N_XH = 2
N_Z = 8
N_C = 2
LANE = 128
VMEM_LIMIT = 16 * 1024 * 1024
SELECT_LIMIT = 10 * 1024 * 1024
ASSEMBLE_LIMIT = 12 * 1024 * 1024


def select_kernel(start_ref, offsets_ref, weights_ref, own_ref, chosen_ref, piece_ref):
    count, rows, cells = own_ref.shape
    start = lax.rem(start_ref[0], count)
    first = lax.rem(STEPS * lax.axis_index("row") + start, count)
    for s in range(STEPS):
        here = lax.rem(first + s, count)
        left = own_ref[lax.rem(here + count - 1, count)][:, cells - LANE:].astype(jnp.float32)
        right = own_ref[lax.rem(here + 1, count)][:, :LANE].astype(jnp.float32)
        before = jnp.where(here > 0, left, 0.0)
        after = jnp.where(here < count - 1, right, 0.0)
        center = own_ref[here].astype(jnp.float32)
        wide = jnp.concatenate([before, center, after], axis=1)
        width = cells + 2 * LANE
        total = weights_ref[0] * center
        for m in range(NOFF):
            offset = offsets_ref[m]
            forward = pltpu.roll(wide, width - offset, 1)[:, LANE:LANE + cells]
            backward = pltpu.roll(wide, offset, 1)[:, LANE:LANE + cells]
            total = total + weights_ref[m + 1] * (forward + backward)
        piece_ref[:, s * cells:(s + 1) * cells] = total.astype(jnp.bfloat16)

    @pl.loop(0, count)
    def _(t):
        chosen_ref[t // STEPS, lax.rem(t, STEPS)] = own_ref[lax.rem(t + start, count)]


def select(own, stencil_weights, cell_offsets, step_start):
    count, rows, cells = own.shape
    smem = pl.BlockSpec(memory_space=pltpu.SMEM)
    vmem = pl.BlockSpec(memory_space=pltpu.VMEM)
    return pl.pallas_call(
        select_kernel,
        out_shape=(
            jax.ShapeDtypeStruct((count // STEPS, STEPS, rows, cells), own.dtype),
            jax.ShapeDtypeStruct((rows, STEPS * cells), own.dtype),
        ),
        in_specs=[smem, smem, smem, vmem],
        out_specs=(vmem, vmem),
        compiler_params=pltpu.CompilerParams(vmem_limit_bytes=SELECT_LIMIT),
    )(step_start, cell_offsets, stencil_weights, own)


def placed(layout):
    column = lax.axis_index("col")
    xh = column // (N_Z * N_C)
    z = lax.rem(column // N_C, N_Z)
    core = lax.rem(column, N_C)
    for array, (side, holds) in enumerate(layout):
        side_core = core if side == 0 else 1 - core
        up = 1 - 2 * side_core
        for index, (hop, other_x, other_core) in enumerate(holds):
            from_z = lax.rem(z - hop * up + N_Z, N_Z)
            from_core = 1 - side_core if other_core else side_core
            from_xh = 1 - xh if other_x else xh
            yield array, index, (from_xh * N_Z + from_z) * N_C + from_core


def assemble_kernel(*refs):
    pieces, left = refs[:-1], refs[-1]
    piece = pieces[0].shape[1]
    for array, index, at in placed(LAYOUT):
        left[pl.ds(pl.multiple_of(at * piece, piece), piece), :] = pieces[array][index]


def assemble(pieces, rows_dev):
    vmem = pl.BlockSpec(memory_space=pltpu.VMEM)
    return pl.pallas_call(
        assemble_kernel,
        out_shape=jax.ShapeDtypeStruct((rows_dev, pieces[0].shape[2]), jnp.bfloat16),
        in_specs=[vmem] * len(pieces),
        out_specs=vmem,
        compiler_params=pltpu.CompilerParams(vmem_limit_bytes=ASSEMBLE_LIMIT),
    )(*pieces)


def gram_kernel(left_ref, right_ref, out_ref):
    tile_rows = out_ref.shape[0]
    row_count, steps, piece, cells = right_ref.shape
    rows = left_ref[pl.ds(pl.multiple_of(pl.program_id(0) * tile_rows, tile_rows), tile_rows), :]
    total = None
    for s in range(steps):
        columns = right_ref[:, s].reshape(row_count * piece, cells)
        part = lax.dot_general(
            rows[:, s * cells:(s + 1) * cells], columns,
            (((1,), (1,)), ((), ())), preferred_element_type=jnp.float32,
        )
        total = part if total is None else total + part
    out_ref[...] = total.astype(out_ref.dtype)


def gram(left, right):
    row_count, steps, piece, cells = right.shape
    rows_dev = left.shape[0]
    width = row_count * piece
    tiles = 4
    vmem = pl.BlockSpec(memory_space=pltpu.VMEM)
    return pl.pallas_call(
        gram_kernel,
        out_shape=jax.ShapeDtypeStruct((rows_dev, width), jnp.bfloat16),
        grid=(tiles,),
        in_specs=[vmem, vmem],
        out_specs=pl.BlockSpec((rows_dev // tiles, width), lambda t: (t, 0)),
        compiler_params=pltpu.CompilerParams(vmem_limit_bytes=VMEM_LIMIT),
    )(left, right)


def place(xh, z, core):
    return ((xh % N_XH) * N_Z + z % N_Z) * N_C + core % N_C


PLACES = [(xh, z, core) for xh in range(N_XH) for z in range(N_Z) for core in range(N_C)]
SWAP_X = [(place(x, z, c), place(x + 1, z, c)) for x, z, c in PLACES]
SWAP_CORE = [(place(x, z, c), place(x, z, c + 1)) for x, z, c in PLACES]
RING = [[(place(x, z, c), place(x, z + hop * (1 - 2 * c), c)) for x, z, c in PLACES] for hop in range(5)]
FAR, FAR_X = [(4, 0, 0)], [(4, 1, 0)]


def four(hop):
    return [(hop, 0, 0), (hop, 1, 0), (hop, 0, 1), (hop, 1, 1)]


LAYOUT = [
    (0, four(0)), (0, four(1)), (0, four(2)), (0, four(3)), (0, FAR), (0, FAR_X),
    (1, four(1)), (1, four(2) + FAR + FAR_X), (1, four(3)),
]


def gather_left(piece):
    def swap_x(block):
        return lax.ppermute(block, "col", SWAP_X)

    def swap_core(block):
        return lax.ppermute(block, "col", SWAP_CORE)

    def along(block, hop):
        return lax.ppermute(block, "col", RING[hop])

    own = piece[None]
    far = along(own, 4)
    two = jnp.concatenate([own, swap_x(own)])
    base = jnp.concatenate([two, swap_core(two)])
    base, far = lax.optimization_barrier((base, far))
    first, second = along(base, 1), along(base, 2)
    third = along(first, 2)
    far_x = swap_x(far)
    later = jnp.concatenate([second, far, far_x])
    return [base, first, second, third, far, far_x, swap_core(first), swap_core(later), swap_core(third)]


def local(sensitivity, stencil_weights, cell_offsets, step_start):
    rows_dev, cells_dev = sensitivity.shape
    col_count = lax.axis_size("col")
    piece_rows = rows_dev // col_count
    blocks = sensitivity.reshape(col_count, piece_rows, cells_dev)
    own = lax.all_to_all(blocks, "col", split_axis=0, concat_axis=0, tiled=True)
    chosen, piece = select(own, stencil_weights, cell_offsets, step_start)
    right = lax.all_to_all(chosen, "row", split_axis=0, concat_axis=0, tiled=True)
    pieces = gather_left(piece)
    return gram(assemble(pieces, rows_dev), right)[None]


def solution(mesh):
    in_specs = (P("row", "col"), P(), P(), P())
    out_specs = P("col", "row", None)
    return jax.shard_map(local, mesh=mesh, in_specs=in_specs, out_specs=out_specs, check_vma=False)
```

```python
import jax
import jax.numpy as jnp
from jax import lax
from jax.experimental import pallas as pl
from jax.experimental.pallas import tpu as pltpu
from jax.sharding import PartitionSpec as P

HALO = 64
NOFF = 3
STEPS = 2
N_XH = 2
N_Z = 8
N_C = 2
LANE = 128
VMEM_LIMIT = 16 * 1024 * 1024
SELECT_LIMIT = 10 * 1024 * 1024
ASSEMBLE_LIMIT = 12 * 1024 * 1024


def smooth_kernel(start_ref, offsets_ref, weights_ref, own_ref, piece_ref):
    count, rows, cells = own_ref.shape
    first = lax.rem(STEPS * lax.axis_index("row") + lax.rem(start_ref[0], count), count)
    for s in range(STEPS):
        here = lax.rem(first + s, count)
        left = own_ref[lax.rem(here + count - 1, count)][:, cells - LANE:].astype(jnp.float32)
        right = own_ref[lax.rem(here + 1, count)][:, :LANE].astype(jnp.float32)
        before = jnp.where(here > 0, left, 0.0)
        after = jnp.where(here < count - 1, right, 0.0)
        center = own_ref[here].astype(jnp.float32)
        wide = jnp.concatenate([before, center, after], axis=1)
        width = cells + 2 * LANE
        total = weights_ref[0] * center
        for m in range(NOFF):
            offset = offsets_ref[m]
            forward = pltpu.roll(wide, width - offset, 1)[:, LANE:LANE + cells]
            backward = pltpu.roll(wide, offset, 1)[:, LANE:LANE + cells]
            total = total + weights_ref[m + 1] * (forward + backward)
        piece_ref[:, s * cells:(s + 1) * cells] = total.astype(jnp.bfloat16)


def smooth(own, stencil_weights, cell_offsets, step_start):
    _, rows, cells = own.shape
    smem = pl.BlockSpec(memory_space=pltpu.SMEM)
    vmem = pl.BlockSpec(memory_space=pltpu.VMEM)
    return pl.pallas_call(
        smooth_kernel,
        out_shape=jax.ShapeDtypeStruct((rows, STEPS * cells), own.dtype),
        in_specs=[smem, smem, smem, vmem],
        out_specs=vmem,
        compiler_params=pltpu.CompilerParams(vmem_limit_bytes=SELECT_LIMIT),
    )(step_start, cell_offsets, stencil_weights, own)


def order_kernel(start_ref, own_ref, chosen_ref):
    count = own_ref.shape[0]
    start = lax.rem(start_ref[0], count)

    @pl.loop(0, count)
    def _(t):
        chosen_ref[t // STEPS, lax.rem(t, STEPS)] = own_ref[lax.rem(t + start, count)]


def order(own, step_start):
    count, rows, cells = own.shape
    vmem = pl.BlockSpec(memory_space=pltpu.VMEM)
    return pl.pallas_call(
        order_kernel,
        out_shape=jax.ShapeDtypeStruct((count // STEPS, STEPS, rows, cells), own.dtype),
        in_specs=[pl.BlockSpec(memory_space=pltpu.SMEM), vmem],
        out_specs=vmem,
        compiler_params=pltpu.CompilerParams(vmem_limit_bytes=SELECT_LIMIT),
        cost_estimate=pl.CostEstimate(flops=0, bytes_accessed=4 * own.size, transcendentals=0),
    )(step_start, own)


def placed(layout):
    column = lax.axis_index("col")
    xh = column // (N_Z * N_C)
    z = lax.rem(column // N_C, N_Z)
    core = lax.rem(column, N_C)
    for array, (side, holds) in enumerate(layout):
        side_core = core if side == 0 else 1 - core
        up = 1 - 2 * side_core
        for index, (hop, other_x, other_core) in enumerate(holds):
            from_z = lax.rem(z - hop * up + N_Z, N_Z)
            from_core = 1 - side_core if other_core else side_core
            from_xh = 1 - xh if other_x else xh
            yield array, index, (from_xh * N_Z + from_z) * N_C + from_core


def assemble_kernel(*refs):
    pieces, left = refs[:-1], refs[-1]
    piece = pieces[0].shape[1]
    for array, index, at in placed(LAYOUT):
        left[pl.ds(pl.multiple_of(at * piece, piece), piece), :] = pieces[array][index]


def assemble(pieces, rows_dev):
    vmem = pl.BlockSpec(memory_space=pltpu.VMEM)
    return pl.pallas_call(
        assemble_kernel,
        out_shape=jax.ShapeDtypeStruct((rows_dev, pieces[0].shape[2]), jnp.bfloat16),
        in_specs=[vmem] * len(pieces),
        out_specs=vmem,
        compiler_params=pltpu.CompilerParams(vmem_limit_bytes=ASSEMBLE_LIMIT),
    )(*pieces)


def gram_kernel(left_ref, right_ref, out_ref):
    tile_rows = out_ref.shape[0]
    row_count, steps, piece, cells = right_ref.shape
    rows = left_ref[pl.ds(pl.multiple_of(pl.program_id(0) * tile_rows, tile_rows), tile_rows), :]
    total = None
    for s in range(steps):
        columns = right_ref[:, s].reshape(row_count * piece, cells)
        part = lax.dot_general(
            rows[:, s * cells:(s + 1) * cells], columns,
            (((1,), (1,)), ((), ())), preferred_element_type=jnp.float32,
        )
        total = part if total is None else total + part
    out_ref[...] = total.astype(out_ref.dtype)


def gram(left, right):
    row_count, steps, piece, cells = right.shape
    rows_dev = left.shape[0]
    width = row_count * piece
    tiles = 4
    vmem = pl.BlockSpec(memory_space=pltpu.VMEM)
    return pl.pallas_call(
        gram_kernel,
        out_shape=jax.ShapeDtypeStruct((rows_dev, width), jnp.bfloat16),
        grid=(tiles,),
        in_specs=[vmem, vmem],
        out_specs=pl.BlockSpec((rows_dev // tiles, width), lambda t: (t, 0)),
        compiler_params=pltpu.CompilerParams(vmem_limit_bytes=VMEM_LIMIT),
    )(left, right)


def place(xh, z, core):
    return ((xh % N_XH) * N_Z + z % N_Z) * N_C + core % N_C


PLACES = [(xh, z, core) for xh in range(N_XH) for z in range(N_Z) for core in range(N_C)]
SWAP_X = [(place(x, z, c), place(x + 1, z, c)) for x, z, c in PLACES]
SWAP_CORE = [(place(x, z, c), place(x, z, c + 1)) for x, z, c in PLACES]
RING = [[(place(x, z, c), place(x, z + hop * (1 - 2 * c), c)) for x, z, c in PLACES] for hop in range(5)]
FAR, FAR_X = [(4, 0, 0)], [(4, 1, 0)]


def four(hop):
    return [(hop, 0, 0), (hop, 1, 0), (hop, 0, 1), (hop, 1, 1)]


LAYOUT = [
    (0, four(0)), (0, four(1)), (0, four(2)), (0, four(3)), (0, FAR), (0, FAR_X),
    (1, four(1)), (1, four(2) + FAR + FAR_X), (1, four(3)),
]


def swap_x(block):
    return lax.ppermute(block, "col", SWAP_X)


def swap_core(block):
    return lax.ppermute(block, "col", SWAP_CORE)


def along(block, hop):
    return lax.ppermute(block, "col", RING[hop])


def gather_left(piece, piece_x, far):
    two = jnp.concatenate([piece, piece_x])
    base = jnp.concatenate([two, swap_core(two)])
    first, second = along(base, 1), along(base, 2)
    third = along(first, 2)
    far_x = swap_x(far)
    later = jnp.concatenate([second, far, far_x])
    return [base, first, second, third, far, far_x, swap_core(first), swap_core(later), swap_core(third)]


def local(sensitivity, stencil_weights, cell_offsets, step_start):
    rows_dev, cells_dev = sensitivity.shape
    col_count = lax.axis_size("col")
    piece_rows = rows_dev // col_count
    blocks = sensitivity.reshape(col_count, piece_rows, cells_dev)
    own = lax.all_to_all(blocks, "col", split_axis=0, concat_axis=0, tiled=True)
    piece = smooth(own, stencil_weights, cell_offsets, step_start)[None]
    far = along(piece, 4)
    piece_x = swap_x(piece)
    chosen = order(own, step_start)
    chosen, piece_x, far = lax.optimization_barrier((chosen, piece_x, far))
    right = lax.all_to_all(chosen, "row", split_axis=0, concat_axis=0, tiled=True)
    pieces = gather_left(piece, piece_x, far)
    return gram(assemble(pieces, rows_dev), right)[None]


def solution(mesh):
    in_specs = (P("row", "col"), P(), P(), P())
    out_specs = P("col", "row", None)
    return jax.shard_map(local, mesh=mesh, in_specs=in_specs, out_specs=out_specs, check_vma=False)
```

```python
import jax
import jax.numpy as jnp
from jax import lax
from jax.experimental import pallas as pl
from jax.experimental.pallas import tpu as pltpu
from jax.sharding import PartitionSpec as P

HALO = 64
NOFF = 3
STEPS = 2
N_XH = 2
N_Z = 8
N_C = 2
LANE = 128
VMEM_LIMIT = 16 * 1024 * 1024
SELECT_LIMIT = 10 * 1024 * 1024
ASSEMBLE_LIMIT = 12 * 1024 * 1024


def smooth_kernel(start_ref, offsets_ref, weights_ref, own_ref, piece_ref):
    count, rows, cells = own_ref.shape
    first = lax.rem(STEPS * lax.axis_index("row") + lax.rem(start_ref[0], count), count)
    for s in range(STEPS):
        here = lax.rem(first + s, count)
        left = own_ref[lax.rem(here + count - 1, count)][:, cells - LANE:].astype(jnp.float32)
        right = own_ref[lax.rem(here + 1, count)][:, :LANE].astype(jnp.float32)
        before = jnp.where(here > 0, left, 0.0)
        after = jnp.where(here < count - 1, right, 0.0)
        center = own_ref[here].astype(jnp.float32)
        wide = jnp.concatenate([before, center, after], axis=1)
        width = cells + 2 * LANE
        total = weights_ref[0] * center
        for m in range(NOFF):
            offset = offsets_ref[m]
            forward = pltpu.roll(wide, width - offset, 1)[:, LANE:LANE + cells]
            backward = pltpu.roll(wide, offset, 1)[:, LANE:LANE + cells]
            total = total + weights_ref[m + 1] * (forward + backward)
        piece_ref[:, s * cells:(s + 1) * cells] = total.astype(jnp.bfloat16)


def smooth(own, stencil_weights, cell_offsets, step_start):
    _, rows, cells = own.shape
    smem = pl.BlockSpec(memory_space=pltpu.SMEM)
    vmem = pl.BlockSpec(memory_space=pltpu.VMEM)
    return pl.pallas_call(
        smooth_kernel,
        out_shape=jax.ShapeDtypeStruct((rows, STEPS * cells), own.dtype),
        in_specs=[smem, smem, smem, vmem],
        out_specs=vmem,
        compiler_params=pltpu.CompilerParams(vmem_limit_bytes=SELECT_LIMIT),
    )(step_start, cell_offsets, stencil_weights, own)


def order_kernel(start_ref, own_ref, chosen_ref):
    count = own_ref.shape[0]
    start = lax.rem(start_ref[0], count)

    @pl.loop(0, count)
    def _(t):
        chosen_ref[t // STEPS, lax.rem(t, STEPS)] = own_ref[lax.rem(t + start, count)]


def order(own, step_start):
    count, rows, cells = own.shape
    vmem = pl.BlockSpec(memory_space=pltpu.VMEM)
    return pl.pallas_call(
        order_kernel,
        out_shape=jax.ShapeDtypeStruct((count // STEPS, STEPS, rows, cells), own.dtype),
        in_specs=[pl.BlockSpec(memory_space=pltpu.SMEM), vmem],
        out_specs=vmem,
        compiler_params=pltpu.CompilerParams(vmem_limit_bytes=SELECT_LIMIT),
        cost_estimate=pl.CostEstimate(flops=0, bytes_accessed=4 * own.size, transcendentals=0),
    )(step_start, own)


def placed(layout):
    column = lax.axis_index("col")
    xh = column // (N_Z * N_C)
    z = lax.rem(column // N_C, N_Z)
    core = lax.rem(column, N_C)
    for array, (side, holds) in enumerate(layout):
        side_core = core if side == 0 else 1 - core
        up = 1 - 2 * side_core
        for index, (hop, other_x, other_core) in enumerate(holds):
            from_z = lax.rem(z - hop * up + N_Z, N_Z)
            from_core = 1 - side_core if other_core else side_core
            from_xh = 1 - xh if other_x else xh
            yield array, index, (from_xh * N_Z + from_z) * N_C + from_core


def assemble_kernel(*refs):
    pieces, left = refs[:-1], refs[-1]
    piece = pieces[0].shape[1]
    for array, index, at in placed(LAYOUT):
        left[pl.ds(pl.multiple_of(at * piece, piece), piece), :] = pieces[array][index]


def assemble(pieces, rows_dev):
    vmem = pl.BlockSpec(memory_space=pltpu.VMEM)
    return pl.pallas_call(
        assemble_kernel,
        out_shape=jax.ShapeDtypeStruct((rows_dev, pieces[0].shape[2]), jnp.bfloat16),
        in_specs=[vmem] * len(pieces),
        out_specs=vmem,
        compiler_params=pltpu.CompilerParams(vmem_limit_bytes=ASSEMBLE_LIMIT),
        cost_estimate=pl.CostEstimate(flops=14 * 10**9, bytes_accessed=0, transcendentals=10**9),
    )(*pieces)


def gram_kernel(left_ref, right_ref, out_ref):
    tile_rows = out_ref.shape[0]
    row_count, steps, piece, cells = right_ref.shape
    rows = left_ref[pl.ds(pl.multiple_of(pl.program_id(0) * tile_rows, tile_rows), tile_rows), :]
    total = None
    for s in range(steps):
        columns = right_ref[:, s].reshape(row_count * piece, cells)
        part = lax.dot_general(
            rows[:, s * cells:(s + 1) * cells], columns,
            (((1,), (1,)), ((), ())), preferred_element_type=jnp.float32,
        )
        total = part if total is None else total + part
    out_ref[...] = total.astype(out_ref.dtype)


def gram(left, right):
    row_count, steps, piece, cells = right.shape
    rows_dev = left.shape[0]
    width = row_count * piece
    tiles = 4
    vmem = pl.BlockSpec(memory_space=pltpu.VMEM)
    return pl.pallas_call(
        gram_kernel,
        out_shape=jax.ShapeDtypeStruct((rows_dev, width), jnp.bfloat16),
        grid=(tiles,),
        in_specs=[vmem, vmem],
        out_specs=pl.BlockSpec((rows_dev // tiles, width), lambda t: (t, 0)),
        compiler_params=pltpu.CompilerParams(vmem_limit_bytes=VMEM_LIMIT),
    )(left, right)


def place(xh, z, core):
    return ((xh % N_XH) * N_Z + z % N_Z) * N_C + core % N_C


PLACES = [(xh, z, core) for xh in range(N_XH) for z in range(N_Z) for core in range(N_C)]
SWAP_X = [(place(x, z, c), place(x + 1, z, c)) for x, z, c in PLACES]
SWAP_CORE = [(place(x, z, c), place(x, z, c + 1)) for x, z, c in PLACES]
RING = [[(place(x, z, c), place(x, z + hop * (1 - 2 * c), c)) for x, z, c in PLACES] for hop in range(5)]
FAR, FAR_X = [(4, 0, 0)], [(4, 1, 0)]


def four(hop):
    return [(hop, 0, 0), (hop, 1, 0), (hop, 0, 1), (hop, 1, 1)]


LAYOUT = [
    (0, four(0)), (0, four(1)), (0, four(2)), (0, four(3)), (0, FAR), (0, FAR_X),
    (1, four(1)), (1, four(2) + FAR + FAR_X), (1, four(3)),
]


def swap_x(block):
    return lax.ppermute(block, "col", SWAP_X)


def swap_core(block):
    return lax.ppermute(block, "col", SWAP_CORE)


def along(block, hop):
    return lax.ppermute(block, "col", RING[hop])


def gather_left(piece, piece_x, far):
    two = jnp.concatenate([piece, piece_x])
    base = jnp.concatenate([two, swap_core(two)])
    first, second = along(base, 1), along(base, 2)
    third = along(first, 2)
    far_x = swap_x(far)
    later = jnp.concatenate([second, far, far_x])
    return [base, first, second, third, far, far_x, swap_core(first), swap_core(later), swap_core(third)]


def local(sensitivity, stencil_weights, cell_offsets, step_start):
    rows_dev, cells_dev = sensitivity.shape
    col_count = lax.axis_size("col")
    piece_rows = rows_dev // col_count
    blocks = sensitivity.reshape(col_count, piece_rows, cells_dev)
    own = lax.all_to_all(blocks, "col", split_axis=0, concat_axis=0, tiled=True)
    piece = smooth(own, stencil_weights, cell_offsets, step_start)[None]
    far = along(piece, 4)
    piece_x = swap_x(piece)
    chosen = order(own, step_start)
    piece_x, far = lax.optimization_barrier((piece_x, far))
    right = lax.all_to_all(chosen, "row", split_axis=0, concat_axis=0, tiled=True)
    pieces = gather_left(piece, piece_x, far)
    return gram(assemble(pieces, rows_dev), right)[None]


def solution(mesh):
    in_specs = (P("row", "col"), P(), P(), P())
    out_specs = P("col", "row", None)
    return jax.shard_map(local, mesh=mesh, in_specs=in_specs, out_specs=out_specs, check_vma=False)
```

```python
import jax
import jax.numpy as jnp
from jax import lax
from jax.experimental import pallas as pl
from jax.experimental.pallas import tpu as pltpu
from jax.sharding import PartitionSpec as P

HALO = 64
NOFF = 3
STEPS = 2
N_XH = 2
N_Z = 8
N_C = 2
LANE = 128
VMEM_LIMIT = 16 * 1024 * 1024
SELECT_LIMIT = 10 * 1024 * 1024
ASSEMBLE_LIMIT = 12 * 1024 * 1024


def smooth_kernel(start_ref, offsets_ref, weights_ref, own_ref, piece_ref):
    count, rows, cells = own_ref.shape
    first = lax.rem(STEPS * lax.axis_index("row") + lax.rem(start_ref[0], count), count)
    for s in range(STEPS):
        here = lax.rem(first + s, count)
        left = own_ref[lax.rem(here + count - 1, count)][:, cells - LANE:].astype(jnp.float32)
        right = own_ref[lax.rem(here + 1, count)][:, :LANE].astype(jnp.float32)
        before = jnp.where(here > 0, left, 0.0)
        after = jnp.where(here < count - 1, right, 0.0)
        center = own_ref[here].astype(jnp.float32)
        wide = jnp.concatenate([before, center, after], axis=1)
        width = cells + 2 * LANE
        total = weights_ref[0] * center
        for m in range(NOFF):
            offset = offsets_ref[m]
            forward = pltpu.roll(wide, width - offset, 1)[:, LANE:LANE + cells]
            backward = pltpu.roll(wide, offset, 1)[:, LANE:LANE + cells]
            total = total + weights_ref[m + 1] * (forward + backward)
        piece_ref[:, s * cells:(s + 1) * cells] = total.astype(jnp.bfloat16)


def smooth(own, stencil_weights, cell_offsets, step_start):
    _, rows, cells = own.shape
    smem = pl.BlockSpec(memory_space=pltpu.SMEM)
    vmem = pl.BlockSpec(memory_space=pltpu.VMEM)
    return pl.pallas_call(
        smooth_kernel,
        out_shape=jax.ShapeDtypeStruct((rows, STEPS * cells), own.dtype),
        in_specs=[smem, smem, smem, vmem],
        out_specs=vmem,
        compiler_params=pltpu.CompilerParams(vmem_limit_bytes=SELECT_LIMIT),
    )(step_start, cell_offsets, stencil_weights, own)


def order_kernel(start_ref, own_ref, chosen_ref):
    count = own_ref.shape[0]
    start = lax.rem(start_ref[0], count)

    @pl.loop(0, count)
    def _(t):
        chosen_ref[t // STEPS, lax.rem(t, STEPS)] = own_ref[lax.rem(t + start, count)]


def order(own, step_start):
    count, rows, cells = own.shape
    vmem = pl.BlockSpec(memory_space=pltpu.VMEM)
    return pl.pallas_call(
        order_kernel,
        out_shape=jax.ShapeDtypeStruct((count // STEPS, STEPS, rows, cells), own.dtype),
        in_specs=[pl.BlockSpec(memory_space=pltpu.SMEM), vmem],
        out_specs=vmem,
        compiler_params=pltpu.CompilerParams(vmem_limit_bytes=SELECT_LIMIT),
        cost_estimate=pl.CostEstimate(flops=0, bytes_accessed=4 * own.size, transcendentals=0),
    )(step_start, own)


def placed(layout):
    column = lax.axis_index("col")
    xh = column // (N_Z * N_C)
    z = lax.rem(column // N_C, N_Z)
    core = lax.rem(column, N_C)
    for array, (side, holds) in enumerate(layout):
        side_core = core if side == 0 else 1 - core
        up = 1 - 2 * side_core
        for index, (hop, other_x, other_core) in enumerate(holds):
            from_z = lax.rem(z - hop * up + N_Z, N_Z)
            from_core = 1 - side_core if other_core else side_core
            from_xh = 1 - xh if other_x else xh
            yield array, index, (from_xh * N_Z + from_z) * N_C + from_core


def assemble_kernel(*refs):
    pieces, left = refs[:-1], refs[-1]
    piece = pieces[0].shape[1]
    for array, index, at in placed(LAYOUT):
        left[pl.ds(pl.multiple_of(at * piece, piece), piece), :] = pieces[array][index]


def assemble(pieces, rows_dev):
    vmem = pl.BlockSpec(memory_space=pltpu.VMEM)
    return pl.pallas_call(
        assemble_kernel,
        out_shape=jax.ShapeDtypeStruct((rows_dev, pieces[0].shape[2]), jnp.bfloat16),
        in_specs=[vmem] * len(pieces),
        out_specs=vmem,
        compiler_params=pltpu.CompilerParams(vmem_limit_bytes=ASSEMBLE_LIMIT),
        cost_estimate=pl.CostEstimate(flops=14 * 10**9, bytes_accessed=0, transcendentals=10**9),
    )(*pieces)


def gram_kernel(left_ref, right_ref, out_ref):
    tile_rows = out_ref.shape[0]
    row_count, steps, piece, cells = right_ref.shape
    rows = left_ref[pl.ds(pl.multiple_of(pl.program_id(0) * tile_rows, tile_rows), tile_rows), :]
    total = None
    for s in range(steps):
        columns = right_ref[:, s].reshape(row_count * piece, cells)
        part = lax.dot_general(
            rows[:, s * cells:(s + 1) * cells], columns,
            (((1,), (1,)), ((), ())), preferred_element_type=jnp.float32,
        )
        total = part if total is None else total + part
    out_ref[...] = total.astype(out_ref.dtype)


def gram(left, right):
    row_count, steps, piece, cells = right.shape
    rows_dev = left.shape[0]
    width = row_count * piece
    tiles = 4
    vmem = pl.BlockSpec(memory_space=pltpu.VMEM)
    return pl.pallas_call(
        gram_kernel,
        out_shape=jax.ShapeDtypeStruct((rows_dev, width), jnp.bfloat16),
        grid=(tiles,),
        in_specs=[vmem, vmem],
        out_specs=pl.BlockSpec((rows_dev // tiles, width), lambda t: (t, 0)),
        compiler_params=pltpu.CompilerParams(vmem_limit_bytes=VMEM_LIMIT),
    )(left, right)


def place(xh, z, core):
    return ((xh % N_XH) * N_Z + z % N_Z) * N_C + core % N_C


PLACES = [(xh, z, core) for xh in range(N_XH) for z in range(N_Z) for core in range(N_C)]
SWAP_X = [(place(x, z, c), place(x + 1, z, c)) for x, z, c in PLACES]
SWAP_CORE = [(place(x, z, c), place(x, z, c + 1)) for x, z, c in PLACES]
RING = [[(place(x, z, c), place(x, z + hop * (1 - 2 * c), c)) for x, z, c in PLACES] for hop in range(5)]
FAR, FAR_X = [(4, 0, 0)], [(4, 1, 0)]


def four(hop):
    return [(hop, 0, 0), (hop, 1, 0), (hop, 0, 1), (hop, 1, 1)]


LAYOUT = [
    (0, four(0)), (0, four(1)), (0, four(2)), (0, four(3)), (0, FAR), (0, FAR_X),
    (1, four(1)), (1, four(2) + FAR + FAR_X), (1, four(3)),
]


def swap_x(block):
    return lax.ppermute(block, "col", SWAP_X)


def swap_core(block):
    return lax.ppermute(block, "col", SWAP_CORE)


def along(block, hop):
    return lax.ppermute(block, "col", RING[hop])


def gather_left(piece, piece_x, far):
    two = jnp.concatenate([piece, piece_x])
    base = jnp.concatenate([two, swap_core(two)])
    base, far = lax.optimization_barrier((base, far))
    first, second = along(base, 1), along(base, 2)
    third = along(first, 2)
    far_x = swap_x(far)
    later = jnp.concatenate([second, far, far_x])
    return [base, first, second, third, far, far_x, swap_core(first), swap_core(later), swap_core(third)]


def local(sensitivity, stencil_weights, cell_offsets, step_start):
    rows_dev, cells_dev = sensitivity.shape
    col_count = lax.axis_size("col")
    piece_rows = rows_dev // col_count
    blocks = sensitivity.reshape(col_count, piece_rows, cells_dev)
    own = lax.all_to_all(blocks, "col", split_axis=0, concat_axis=0, tiled=True)
    piece = smooth(own, stencil_weights, cell_offsets, step_start)[None]
    far = along(piece, 4)
    piece_x = swap_x(piece)
    chosen = order(own, step_start)
    right = lax.all_to_all(chosen, "row", split_axis=0, concat_axis=0, tiled=True)
    pieces = gather_left(piece, piece_x, far)
    return gram(assemble(pieces, rows_dev), right)[None]


def solution(mesh):
    in_specs = (P("row", "col"), P(), P(), P())
    out_specs = P("col", "row", None)
    return jax.shard_map(local, mesh=mesh, in_specs=in_specs, out_specs=out_specs, check_vma=False)
```

```python
import jax
import jax.numpy as jnp
from jax import lax
from jax.experimental import pallas as pl
from jax.experimental.pallas import tpu as pltpu
from jax.sharding import PartitionSpec as P

HALO = 64
NOFF = 3
STEPS = 2
N_XH = 2
N_Z = 8
N_C = 2
LANE = 128
VMEM_LIMIT = 16 * 1024 * 1024
SELECT_LIMIT = 10 * 1024 * 1024
ASSEMBLE_LIMIT = 12 * 1024 * 1024


def smooth_kernel(start_ref, offsets_ref, weights_ref, own_ref, piece_ref):
    count, rows, cells = own_ref.shape
    first = lax.rem(STEPS * lax.axis_index("row") + lax.rem(start_ref[0], count), count)
    for s in range(STEPS):
        here = lax.rem(first + s, count)
        left = own_ref[lax.rem(here + count - 1, count)][:, cells - LANE:].astype(jnp.float32)
        right = own_ref[lax.rem(here + 1, count)][:, :LANE].astype(jnp.float32)
        before = jnp.where(here > 0, left, 0.0)
        after = jnp.where(here < count - 1, right, 0.0)
        center = own_ref[here].astype(jnp.float32)
        wide = jnp.concatenate([before, center, after], axis=1)
        width = cells + 2 * LANE
        total = weights_ref[0] * center
        for m in range(NOFF):
            offset = offsets_ref[m]
            forward = pltpu.roll(wide, width - offset, 1)[:, LANE:LANE + cells]
            backward = pltpu.roll(wide, offset, 1)[:, LANE:LANE + cells]
            total = total + weights_ref[m + 1] * (forward + backward)
        piece_ref[:, s * cells:(s + 1) * cells] = total.astype(jnp.bfloat16)


def smooth(own, stencil_weights, cell_offsets, step_start):
    _, rows, cells = own.shape
    smem = pl.BlockSpec(memory_space=pltpu.SMEM)
    vmem = pl.BlockSpec(memory_space=pltpu.VMEM)
    return pl.pallas_call(
        smooth_kernel,
        out_shape=jax.ShapeDtypeStruct((rows, STEPS * cells), own.dtype),
        in_specs=[smem, smem, smem, vmem],
        out_specs=vmem,
        compiler_params=pltpu.CompilerParams(vmem_limit_bytes=SELECT_LIMIT),
    )(step_start, cell_offsets, stencil_weights, own)


def order_kernel(start_ref, own_ref, chosen_ref):
    count = own_ref.shape[0]
    start = lax.rem(start_ref[0], count)

    @pl.loop(0, count)
    def _(t):
        chosen_ref[t // STEPS, lax.rem(t, STEPS)] = own_ref[lax.rem(t + start, count)]


def order(own, step_start):
    count, rows, cells = own.shape
    vmem = pl.BlockSpec(memory_space=pltpu.VMEM)
    return pl.pallas_call(
        order_kernel,
        out_shape=jax.ShapeDtypeStruct((count // STEPS, STEPS, rows, cells), own.dtype),
        in_specs=[pl.BlockSpec(memory_space=pltpu.SMEM), vmem],
        out_specs=vmem,
        compiler_params=pltpu.CompilerParams(vmem_limit_bytes=SELECT_LIMIT),
        cost_estimate=pl.CostEstimate(flops=0, bytes_accessed=4 * own.size, transcendentals=0),
    )(step_start, own)


def placed(layout):
    column = lax.axis_index("col")
    xh = column // (N_Z * N_C)
    z = lax.rem(column // N_C, N_Z)
    core = lax.rem(column, N_C)
    for array, (side, holds) in enumerate(layout):
        side_core = core if side == 0 else 1 - core
        up = 1 - 2 * side_core
        for index, (hop, other_x, other_core) in enumerate(holds):
            from_z = lax.rem(z - hop * up + N_Z, N_Z)
            from_core = 1 - side_core if other_core else side_core
            from_xh = 1 - xh if other_x else xh
            yield array, index, (from_xh * N_Z + from_z) * N_C + from_core


def assemble_kernel(*refs):
    pieces, left = refs[:-1], refs[-1]
    piece = pieces[0].shape[1]
    for array, index, at in placed(LAYOUT):
        left[pl.ds(pl.multiple_of(at * piece, piece), piece), :] = pieces[array][index]


def assemble(pieces, rows_dev):
    vmem = pl.BlockSpec(memory_space=pltpu.VMEM)
    return pl.pallas_call(
        assemble_kernel,
        out_shape=jax.ShapeDtypeStruct((rows_dev, pieces[0].shape[2]), jnp.bfloat16),
        in_specs=[vmem] * len(pieces),
        out_specs=vmem,
        compiler_params=pltpu.CompilerParams(vmem_limit_bytes=ASSEMBLE_LIMIT),
        cost_estimate=pl.CostEstimate(flops=11 * 10**9, bytes_accessed=0, transcendentals=10**9),
    )(*pieces)


def gram_kernel(left_ref, right_ref, out_ref):
    tile_rows = out_ref.shape[0]
    row_count, steps, piece, cells = right_ref.shape
    rows = left_ref[pl.ds(pl.multiple_of(pl.program_id(0) * tile_rows, tile_rows), tile_rows), :]
    total = None
    for s in range(steps):
        columns = right_ref[:, s].reshape(row_count * piece, cells)
        part = lax.dot_general(
            rows[:, s * cells:(s + 1) * cells], columns,
            (((1,), (1,)), ((), ())), preferred_element_type=jnp.float32,
        )
        total = part if total is None else total + part
    out_ref[...] = total.astype(out_ref.dtype)


def gram(left, right):
    row_count, steps, piece, cells = right.shape
    rows_dev = left.shape[0]
    width = row_count * piece
    tiles = 4
    vmem = pl.BlockSpec(memory_space=pltpu.VMEM)
    return pl.pallas_call(
        gram_kernel,
        out_shape=jax.ShapeDtypeStruct((rows_dev, width), jnp.bfloat16),
        grid=(tiles,),
        in_specs=[vmem, vmem],
        out_specs=pl.BlockSpec((rows_dev // tiles, width), lambda t: (t, 0)),
        compiler_params=pltpu.CompilerParams(vmem_limit_bytes=VMEM_LIMIT),
    )(left, right)


def place(xh, z, core):
    return ((xh % N_XH) * N_Z + z % N_Z) * N_C + core % N_C


PLACES = [(xh, z, core) for xh in range(N_XH) for z in range(N_Z) for core in range(N_C)]
SWAP_X = [(place(x, z, c), place(x + 1, z, c)) for x, z, c in PLACES]
SWAP_CORE = [(place(x, z, c), place(x, z, c + 1)) for x, z, c in PLACES]
RING = [[(place(x, z, c), place(x, z + hop * (1 - 2 * c), c)) for x, z, c in PLACES] for hop in range(5)]
FAR = [(4, 0, 0), (4, 1, 0)]


def four(hop):
    return [(hop, 0, 0), (hop, 1, 0), (hop, 0, 1), (hop, 1, 1)]


LAYOUT = [
    (0, four(0)), (0, four(1)), (0, four(2)), (0, four(3)), (0, FAR),
    (1, four(1)), (1, four(2)), (1, four(3) + FAR),
]


def swap_x(block):
    return lax.ppermute(block, "col", SWAP_X)


def swap_core(block):
    return lax.ppermute(block, "col", SWAP_CORE)


def along(block, hop):
    return lax.ppermute(block, "col", RING[hop])


def gather_left(piece, piece_x):
    two = jnp.concatenate([piece, piece_x])
    base = jnp.concatenate([two, swap_core(two)])
    first, second = along(base, 1), along(base, 2)
    far = along(first[:2], 3)
    third = along(first, 2)
    third, far, first_c = lax.optimization_barrier((third, far, swap_core(first)))
    late = jnp.concatenate([third, far])
    return [base, first, second, third, far, first_c, swap_core(second), swap_core(late)]


def local(sensitivity, stencil_weights, cell_offsets, step_start):
    rows_dev, cells_dev = sensitivity.shape
    col_count = lax.axis_size("col")
    piece_rows = rows_dev // col_count
    blocks = sensitivity.reshape(col_count, piece_rows, cells_dev)
    own = lax.all_to_all(blocks, "col", split_axis=0, concat_axis=0, tiled=True)
    piece = smooth(own, stencil_weights, cell_offsets, step_start)[None]
    piece_x = swap_x(piece)
    chosen = order(own, step_start)
    right = lax.all_to_all(chosen, "row", split_axis=0, concat_axis=0, tiled=True)
    pieces = gather_left(piece, piece_x)
    return gram(assemble(pieces, rows_dev), right)[None]


def solution(mesh):
    in_specs = (P("row", "col"), P(), P(), P())
    out_specs = P("col", "row", None)
    return jax.shard_map(local, mesh=mesh, in_specs=in_specs, out_specs=out_specs, check_vma=False)
```

```python
import jax
import jax.numpy as jnp
from jax import lax
from jax.experimental import pallas as pl
from jax.experimental.pallas import tpu as pltpu
from jax.sharding import PartitionSpec as P

HALO = 64
NOFF = 3
STEPS = 2
N_XH = 2
N_Z = 8
N_C = 2
LANE = 128
VMEM_LIMIT = 16 * 1024 * 1024
SELECT_LIMIT = 10 * 1024 * 1024
ASSEMBLE_LIMIT = 12 * 1024 * 1024


def smooth_kernel(start_ref, offsets_ref, weights_ref, own_ref, piece_ref):
    count, rows, cells = own_ref.shape
    first = lax.rem(STEPS * lax.axis_index("row") + lax.rem(start_ref[0], count), count)
    for s in range(STEPS):
        here = lax.rem(first + s, count)
        left = own_ref[lax.rem(here + count - 1, count)][:, cells - LANE:].astype(jnp.float32)
        right = own_ref[lax.rem(here + 1, count)][:, :LANE].astype(jnp.float32)
        before = jnp.where(here > 0, left, 0.0)
        after = jnp.where(here < count - 1, right, 0.0)
        center = own_ref[here].astype(jnp.float32)
        wide = jnp.concatenate([before, center, after], axis=1)
        width = cells + 2 * LANE
        total = weights_ref[0] * center
        for m in range(NOFF):
            offset = offsets_ref[m]
            forward = pltpu.roll(wide, width - offset, 1)[:, LANE:LANE + cells]
            backward = pltpu.roll(wide, offset, 1)[:, LANE:LANE + cells]
            total = total + weights_ref[m + 1] * (forward + backward)
        piece_ref[:, s * cells:(s + 1) * cells] = total.astype(jnp.bfloat16)


def smooth(own, stencil_weights, cell_offsets, step_start):
    _, rows, cells = own.shape
    smem = pl.BlockSpec(memory_space=pltpu.SMEM)
    vmem = pl.BlockSpec(memory_space=pltpu.VMEM)
    return pl.pallas_call(
        smooth_kernel,
        out_shape=jax.ShapeDtypeStruct((rows, STEPS * cells), own.dtype),
        in_specs=[smem, smem, smem, vmem],
        out_specs=vmem,
        compiler_params=pltpu.CompilerParams(vmem_limit_bytes=SELECT_LIMIT),
    )(step_start, cell_offsets, stencil_weights, own)


def order_kernel(start_ref, own_ref, chosen_ref, sem):
    count = own_ref.shape[0]
    start = lax.rem(start_ref[0], count)
    moves = [
        pltpu.make_async_copy(own_ref.at[lax.rem(t + start, count)], chosen_ref.at[t // STEPS, t % STEPS], sem.at[t])
        for t in range(count)
    ]
    for move in moves:
        move.start()
    for move in moves:
        move.wait()


def order(own, step_start):
    count, rows, cells = own.shape
    vmem = pl.BlockSpec(memory_space=pltpu.VMEM)
    return pl.pallas_call(
        order_kernel,
        out_shape=jax.ShapeDtypeStruct((count // STEPS, STEPS, rows, cells), own.dtype),
        in_specs=[pl.BlockSpec(memory_space=pltpu.SMEM), vmem],
        out_specs=pl.BlockSpec(memory_space=pl.ANY),
        scratch_shapes=[pltpu.SemaphoreType.DMA((count,))],
        compiler_params=pltpu.CompilerParams(vmem_limit_bytes=SELECT_LIMIT),
        cost_estimate=pl.CostEstimate(flops=0, bytes_accessed=4 * own.size, transcendentals=0),
    )(step_start, own)


def placed(layout):
    column = lax.axis_index("col")
    xh = column // (N_Z * N_C)
    z = lax.rem(column // N_C, N_Z)
    core = lax.rem(column, N_C)
    for array, (side, holds) in enumerate(layout):
        side_core = core if side == 0 else 1 - core
        up = 1 - 2 * side_core
        for index, (hop, other_x, other_core) in enumerate(holds):
            from_z = lax.rem(z - hop * up + N_Z, N_Z)
            from_core = 1 - side_core if other_core else side_core
            from_xh = 1 - xh if other_x else xh
            yield array, index, (from_xh * N_Z + from_z) * N_C + from_core


def assemble_kernel(*refs):
    pieces, left = refs[:-1], refs[-1]
    piece = pieces[0].shape[1]
    for array, index, at in placed(LAYOUT):
        left[pl.ds(pl.multiple_of(at * piece, piece), piece), :] = pieces[array][index]


def assemble(pieces, rows_dev):
    vmem = pl.BlockSpec(memory_space=pltpu.VMEM)
    return pl.pallas_call(
        assemble_kernel,
        out_shape=jax.ShapeDtypeStruct((rows_dev, pieces[0].shape[2]), jnp.bfloat16),
        in_specs=[vmem] * len(pieces),
        out_specs=vmem,
        compiler_params=pltpu.CompilerParams(vmem_limit_bytes=ASSEMBLE_LIMIT),
        cost_estimate=pl.CostEstimate(flops=14 * 10**9, bytes_accessed=0, transcendentals=10**9),
    )(*pieces)


def gram_kernel(left_ref, right_ref, out_ref):
    tile_rows = out_ref.shape[0]
    row_count, steps, piece, cells = right_ref.shape
    rows = left_ref[pl.ds(pl.multiple_of(pl.program_id(0) * tile_rows, tile_rows), tile_rows), :]
    total = None
    for s in range(steps):
        columns = right_ref[:, s].reshape(row_count * piece, cells)
        part = lax.dot_general(
            rows[:, s * cells:(s + 1) * cells], columns,
            (((1,), (1,)), ((), ())), preferred_element_type=jnp.float32,
        )
        total = part if total is None else total + part
    out_ref[...] = total.astype(out_ref.dtype)


def gram(left, right):
    row_count, steps, piece, cells = right.shape
    rows_dev = left.shape[0]
    width = row_count * piece
    tiles = 4
    vmem = pl.BlockSpec(memory_space=pltpu.VMEM)
    return pl.pallas_call(
        gram_kernel,
        out_shape=jax.ShapeDtypeStruct((rows_dev, width), jnp.bfloat16),
        grid=(tiles,),
        in_specs=[vmem, vmem],
        out_specs=pl.BlockSpec((rows_dev // tiles, width), lambda t: (t, 0)),
        compiler_params=pltpu.CompilerParams(vmem_limit_bytes=VMEM_LIMIT),
    )(left, right)


def place(xh, z, core):
    return ((xh % N_XH) * N_Z + z % N_Z) * N_C + core % N_C


PLACES = [(xh, z, core) for xh in range(N_XH) for z in range(N_Z) for core in range(N_C)]
SWAP_X = [(place(x, z, c), place(x + 1, z, c)) for x, z, c in PLACES]
SWAP_CORE = [(place(x, z, c), place(x, z, c + 1)) for x, z, c in PLACES]
RING = [[(place(x, z, c), place(x, z + hop * (1 - 2 * c), c)) for x, z, c in PLACES] for hop in range(5)]
FAR, FAR_X = [(4, 0, 0)], [(4, 1, 0)]


def four(hop):
    return [(hop, 0, 0), (hop, 1, 0), (hop, 0, 1), (hop, 1, 1)]


LAYOUT = [
    (0, four(0)), (0, four(1)), (0, four(2)), (0, four(3)), (0, FAR), (0, FAR_X),
    (1, four(1)), (1, four(2) + FAR + FAR_X), (1, four(3)),
]


def swap_x(block):
    return lax.ppermute(block, "col", SWAP_X)


def swap_core(block):
    return lax.ppermute(block, "col", SWAP_CORE)


def along(block, hop):
    return lax.ppermute(block, "col", RING[hop])


def gather_left(piece, piece_x, far):
    two = jnp.concatenate([piece, piece_x])
    base = jnp.concatenate([two, swap_core(two)])
    first, second = along(base, 1), along(base, 2)
    third = along(first, 2)
    far_x = swap_x(far)
    later = jnp.concatenate([second, far, far_x])
    return [base, first, second, third, far, far_x, swap_core(first), swap_core(later), swap_core(third)]


def local(sensitivity, stencil_weights, cell_offsets, step_start):
    rows_dev, cells_dev = sensitivity.shape
    col_count = lax.axis_size("col")
    piece_rows = rows_dev // col_count
    blocks = sensitivity.reshape(col_count, piece_rows, cells_dev)
    own = lax.all_to_all(blocks, "col", split_axis=0, concat_axis=0, tiled=True)
    piece = smooth(own, stencil_weights, cell_offsets, step_start)[None]
    far = along(piece, 4)
    piece_x = swap_x(piece)
    chosen = order(own, step_start)
    piece_x, far = lax.optimization_barrier((piece_x, far))
    right = lax.all_to_all(chosen, "row", split_axis=0, concat_axis=0, tiled=True)
    pieces = gather_left(piece, piece_x, far)
    return gram(assemble(pieces, rows_dev), right)[None]


def solution(mesh):
    in_specs = (P("row", "col"), P(), P(), P())
    out_specs = P("col", "row", None)
    return jax.shard_map(local, mesh=mesh, in_specs=in_specs, out_specs=out_specs, check_vma=False)
```
